32 devices in a mesh: row: 4 (over x, core), col: 8 (over z, y).
Axes of the slice: x: 2, y: 2, z: 4, core: 2. Of those that a mesh axis runs over, the one named last changes fastest.
Arguments:
- luminance: float32 [512, 4096], P('row', 'col'), may hold values from 0 to 1
- level_gain: float32 [5], replicated, may hold values from 0.5 to 2
Outputs:
- tone_mapped: float32 [512, 4096], P('row', 'col')
The draws below stay inside these ranges and needn't reach their ends.
All inputs are finite; a program needn't handle non-finite values.
Results may differ from the reference program's by a relative error of at most 0.00002.
Values sent between devices are 32-bit elements; how exact they have to be, the bound alone decides.
A program may use at most 64 MiB of HBM per device.

```python
import math
import jax
import jax.numpy as jnp
from jax import lax

CHANNELS = 16
LEVELS = 6
ROWS = 512
COLS = 4096


def block_scale(own_key, extent, split, least, top_value):
    gain = 1.0
    for dim, blocks in split:
        steps = jax.random.uniform(jax.random.fold_in(jax.random.fold_in(own_key, 6), dim), (blocks,), jnp.float32, least / len(split), top_value / len(split))
        gain = gain * jnp.repeat(jnp.exp(steps), extent[dim] // blocks).reshape((-1,) + (1,) * (len(extent) - 1 - dim))
    return gain


def setup_inputs(seed: int = 0) -> dict:
    key_of = jax.random.split(jax.random.key(seed), 3)
    luminance = jnp.clip(1.0 * jax.random.uniform(key_of[0], (ROWS, COLS), jnp.float32) ** block_scale(key_of[0], (ROWS, COLS), ((0, 4), (1, 8)), -0.2, 0.2), 0.0, 1.0)
    level_gain = jnp.clip(jnp.exp(jax.random.uniform(key_of[1], (LEVELS - 1,), jnp.float32, math.log(0.5), math.log(2.0))), 0.5, 2.0)
    return dict(luminance=luminance, level_gain=level_gain)


binomial = (0.0625, 0.25, 0.375, 0.25, 0.0625)
detail_boost = 1.0
base_slope = 0.5
spread_inverse = 1.0 / (2.0 * 0.025 * 0.025)


def remap_tone(values, anchor, switch):
    offset = values - anchor
    return values + switch * ((base_slope - 1.0) * offset + detail_boost * offset * jnp.exp(-offset * offset * spread_inverse))


def hat_weights(guidance, anchor):
    return jnp.maximum(0.0, 1.0 - jnp.abs(guidance - anchor) * (CHANNELS - 1))


def down_valid(padded):
    out_rows = (padded.shape[-2] - 4) // 2
    blurred = binomial[0] * padded[..., 0:2 * out_rows - 1:2, :]
    for step in range(1, 5):
        blurred = blurred + binomial[step] * padded[..., step:step + 2 * out_rows - 1:2, :]
    out_cols = (padded.shape[-1] - 4) // 2
    result = binomial[0] * blurred[..., 0:2 * out_cols - 1:2]
    for step in range(1, 5):
        result = result + binomial[step] * blurred[..., step:step + 2 * out_cols - 1:2]
    return result


def up_valid(coarse):
    rows_in = coarse.shape[-2]
    even_rows = (coarse[..., 0:rows_in - 2, :] + 6.0 * coarse[..., 1:rows_in - 1, :] + coarse[..., 2:rows_in, :]) * 0.125
    odd_rows = (coarse[..., 1:rows_in - 1, :] + coarse[..., 2:rows_in, :]) * 0.5
    joined = jnp.stack([even_rows, odd_rows], axis=-2)
    joined = joined.reshape(joined.shape[:-3] + (2 * (rows_in - 2), joined.shape[-1]))
    cols_in = joined.shape[-1]
    even_cols = (joined[..., 0:cols_in - 2] + 6.0 * joined[..., 1:cols_in - 1] + joined[..., 2:cols_in]) * 0.125
    odd_cols = (joined[..., 1:cols_in - 1] + joined[..., 2:cols_in]) * 0.5
    result = jnp.stack([even_cols, odd_cols], axis=-1)
    return result.reshape(result.shape[:-2] + (2 * (cols_in - 2),))


def down_wrap(values):
    return down_valid(jnp.pad(values, ((2, 2), (2, 2)), mode="wrap"))


def up_wrap(values):
    return up_valid(jnp.pad(values, ((1, 1), (1, 1)), mode="wrap"))


def reference(luminance, level_gain):
    guides = [luminance]
    for level_index in range(LEVELS - 1):
        guides.append(down_wrap(guides[-1]))

    def channel_step(totals, channel_index):
        anchor = channel_index.astype(jnp.float32) / (CHANNELS - 1)
        current = remap_tone(luminance, anchor, 1.0)
        new_totals = []
        for level_index in range(LEVELS - 1):
            coarse = down_wrap(current)
            detail = current - up_wrap(coarse)
            new_totals.append(totals[level_index] + hat_weights(guides[level_index], anchor) * detail)
            current = coarse
        return tuple(new_totals), None

    initial = tuple(jnp.zeros_like(guides[level_index]) for level_index in range(LEVELS - 1))
    totals, unused = lax.scan(channel_step, initial, jnp.arange(CHANNELS, dtype=jnp.int32))
    result = guides[LEVELS - 1]
    for level_index in reversed(range(LEVELS - 1)):
        result = level_gain[level_index] * totals[level_index] + up_wrap(result)
    return result
```

```python
import functools
import jax
import jax.numpy as jnp
import numpy as np
from jax import lax
from jax.experimental import pallas as pl
from jax.experimental.pallas import tpu as pltpu
from jax.sharding import PartitionSpec as P

CHANNELS = 16
LEVELS = 6
HALO_ROWS = 96
HALO_COLS = 128
PAD = 8
LANE = 128

base_slope = 0.5
spread_inverse = 1.0 / (2.0 * 0.025 * 0.025)
MESH = pl.DeviceIdType.MESH


def sizes(block_rows, block_cols):
    rows = [(block_rows + 2 * HALO_ROWS) >> level for level in range(LEVELS)]
    cols = [(block_cols + 2 * HALO_COLS) >> level for level in range(LEVELS)]
    tiles = [-(-c // LANE) for c in cols]
    return rows, cols, tiles


def down_matrix(cols_in, cols_out, tiles_in, tiles_out):
    matrix = np.zeros((tiles_in * LANE, tiles_out * LANE), np.float32)
    for j in range(cols_out):
        for s, weight in enumerate((0.0625, 0.25, 0.375, 0.25, 0.0625)):
            source = 2 * j + s - 2
            if 0 <= source < cols_in:
                matrix[source, j] = weight
    return matrix


def up_matrix(coarse_cols, first, count, tiles_in, tiles_out):
    matrix = np.zeros((tiles_in * LANE, tiles_out * LANE), np.float32)
    for f in range(count):
        m = first + f // 2
        taps = ((m - 1, 0.125), (m, 0.75), (m + 1, 0.125)) if f % 2 == 0 else ((m, 0.5), (m + 1, 0.5))
        for source, weight in taps:
            if 0 <= source < coarse_cols:
                matrix[source, f] = weight
    return matrix


def exchange_kernel(axes, lum, ext, own_sem, send_sem, recv_sem):
    block_rows, block_cols = lum.shape
    row_axis, col_axis = axes
    row, col = lax.axis_index(row_axis), lax.axis_index(col_axis)
    row_count, col_count = lax.axis_size(row_axis), lax.axis_size(col_axis)
    steps = [(dr, dc) for dr in (-1, 0, 1) for dc in (-1, 0, 1) if (dr, dc) != (0, 0)]

    def device(dr, dc):
        return (lax.rem(row + dr + row_count, row_count), lax.rem(col + dc + col_count, col_count))

    barrier = pltpu.get_barrier_semaphore()
    for dr, dc in steps:
        pl.semaphore_signal(barrier, inc=1, device_id=device(dr, dc), device_id_type=MESH)
    own = pltpu.make_async_copy(
        lum, ext.at[pl.ds(HALO_ROWS, block_rows), pl.ds(HALO_COLS, block_cols)], own_sem
    )
    own.start()
    pl.semaphore_wait(barrier, len(steps))

    def span(step, block, halo):
        if step == 0:
            return pl.ds(0, block), pl.ds(halo, block)
        if step < 0:
            return pl.ds(0, halo), pl.ds(halo + block, halo)
        return pl.ds(block - halo, halo), pl.ds(0, halo)

    copies = []
    for index, (dr, dc) in enumerate(steps):
        src_r, dst_r = span(dr, block_rows, HALO_ROWS)
        src_c, dst_c = span(dc, block_cols, HALO_COLS)
        copy = pltpu.make_async_remote_copy(
            src_ref=lum.at[src_r, src_c],
            dst_ref=ext.at[dst_r, dst_c],
            send_sem=send_sem.at[index],
            recv_sem=recv_sem.at[index],
            device_id=device(dr, dc),
            device_id_type=MESH,
        )
        copy.start()
        copies.append(copy)
    own.wait()
    for copy in copies:
        copy.wait()


def exchange(axes, luminance):
    block_rows, block_cols = luminance.shape
    return pl.pallas_call(
        functools.partial(exchange_kernel, axes),
        out_shape=jax.ShapeDtypeStruct(
            (block_rows + 2 * HALO_ROWS, block_cols + 2 * HALO_COLS), jnp.float32
        ),
        in_specs=[pl.BlockSpec(memory_space=pl.ANY)],
        out_specs=pl.BlockSpec(memory_space=pl.ANY),
        scratch_shapes=[
            pltpu.SemaphoreType.DMA,
            pltpu.SemaphoreType.DMA((8,)),
            pltpu.SemaphoreType.DMA((8,)),
        ],
        compiler_params=pltpu.CompilerParams(collective_id=0, has_side_effects=True),
        name="halo_exchange",
    )(luminance)


def mm(x, matrix):
    high = x.astype(jnp.bfloat16)
    low = (x - high.astype(jnp.float32)).astype(jnp.bfloat16)
    return jnp.dot(high, matrix, preferred_element_type=jnp.float32) + jnp.dot(
        low, matrix, preferred_element_type=jnp.float32
    )


def remap_tone(values, anchor):
    offset = values - anchor
    return values + ((base_slope - 1.0) * offset + offset * jnp.exp(-offset * offset * spread_inverse))


def hat(guidance, anchor):
    return jnp.maximum(0.0, 1.0 - jnp.abs(guidance - anchor) * (CHANNELS - 1))


def wide(parts):
    return parts[0] if len(parts) == 1 else jnp.concatenate(parts, axis=1)


def lane(t):
    return slice(t * LANE, (t + 1) * LANE)


def row_down(ref, t, start, count):
    def tap(s):
        return ref[t, pl.ds(start + s - 2, count, stride=2), :]

    return 0.375 * tap(2) + 0.25 * (tap(1) + tap(3)) + 0.0625 * (tap(0) + tap(4))


def row_up(ref, t, start, count):
    before = ref[t, pl.ds(start - 1, count), :]
    here = ref[t, pl.ds(start, count), :]
    after = ref[t, pl.ds(start + 1, count), :]
    return (before + 6.0 * here + after) * 0.125, (here + after) * 0.5


def tone_kernel(rows, tiles, block_rows, block_cols, *refs):
    gain, anchors, lum = refs[:3]
    down = refs[3:8]
    up = refs[8:13]
    out = refs[13]
    center, remapped, first, total, result = refs[14:19]
    stack = (None,) + refs[19:24]
    joined, widened = refs[24:29], refs[29:34]
    collapsed = (None,) + refs[34:39]
    half = block_rows // 2
    own_tiles = block_cols // LANE
    side = HALO_COLS // LANE
    coarse_at = PAD + HALO_ROWS // 2

    for t in range(own_tiles):
        center[t, :, :] = lum[HALO_ROWS : HALO_ROWS + block_rows, lane(side + t)]
    total[...] = jnp.zeros_like(total)

    def shrink(dst_row):
        x = wide([row_down(remapped, t, PAD, rows[1]) for t in range(tiles[0])])
        y = mm(x, down[0][...])
        for t in range(tiles[1]):
            stack[1][t, pl.ds(dst_row, rows[1]), :] = y[:, lane(t)]
        return y

    def channel(k, carry):
        anchor = anchors[k]
        for t in range(tiles[0]):
            for r in range(0, rows[0], 64):
                remapped[t, PAD + r : PAD + r + 64, :] = remap_tone(lum[r : r + 64, lane(t)], anchor)
        y = shrink(pl.multiple_of(PAD + k * rows[1], 8))
        for t in range(tiles[1]):
            first[t, PAD : PAD + rows[1], :] = y[:, lane(t)]
        pairs = [row_up(first, t, coarse_at, half) for t in range(tiles[1])]
        x = jnp.concatenate([wide([p[0] for p in pairs]), wide([p[1] for p in pairs])], axis=0)
        fine = mm(x, up[0][...])
        for t in range(own_tiles):
            for p in range(2):
                guidance = center[t, pl.ds(p, half, stride=2), :]
                value = remapped[side + t, pl.ds(PAD + HALO_ROWS + p, half, stride=2), :]
                total[t, p * half : (p + 1) * half, :] += hat(guidance, anchor) * (
                    value - fine[p * half : (p + 1) * half, lane(t)]
                )
        return carry

    lax.fori_loop(0, CHANNELS, channel, 0)
    for t in range(tiles[0]):
        for r in range(0, rows[0], 64):
            remapped[t, PAD + r : PAD + r + 64, :] = lum[r : r + 64, lane(t)]
    shrink(PAD + CHANNELS * rows[1])

    for level in range(1, LEVELS - 1):
        count = (CHANNELS + 1) * rows[level + 1]
        chunk = count // 5 if count % 40 == 0 else count
        for o in range(0, count, chunk):
            x = wide([row_down(stack[level], t, PAD + 2 * o, chunk) for t in range(tiles[level])])
            y = mm(x, down[level][...])
            for t in range(tiles[level + 1]):
                stack[level + 1][t, PAD + o : PAD + o + chunk, :] = y[:, lane(t)]

    coefficients = [None] * LEVELS
    low = [0, 40, 0, 0, 0]
    high = [0, 120] + rows[2:5]
    for level in range(1, LEVELS - 1):
        fine, coarse = rows[level], rows[level + 1]
        chunk = coarse if coarse % 8 == 0 else CHANNELS * coarse
        spread, wider = joined[level], widened[level]
        for o in range(0, CHANNELS * coarse, chunk):
            for t in range(tiles[level + 1]):
                even, odd = row_up(stack[level + 1], t, PAD + o, chunk)
                spread[t, pl.ds(2 * o, chunk, stride=2), :] = even
                spread[t, pl.ds(2 * o + 1, chunk, stride=2), :] = odd
            x = wide([spread[t, 2 * o : 2 * (o + chunk), :] for t in range(tiles[level + 1])])
            y = mm(x, up[level][...])
            for t in range(tiles[level]):
                wider[t, 2 * o : 2 * (o + chunk), :] = y[:, lane(t)]
        a, b = low[level], high[level]
        sums = []
        for t in range(tiles[level]):
            guidance = stack[level][t, PAD + CHANNELS * fine + a : PAD + CHANNELS * fine + b, :]
            running = None
            for k in range(CHANNELS):
                anchor = np.float32(k) / np.float32(CHANNELS - 1)
                term = hat(guidance, anchor) * (
                    stack[level][t, PAD + k * fine + a : PAD + k * fine + b, :]
                    - wider[t, k * fine + a : k * fine + b, :]
                )
                running = term if running is None else running + term
            sums.append(gain[level] * running)
        coefficients[level] = sums

    last = LEVELS - 1
    guide_at = PAD + CHANNELS * rows[last]
    for t in range(tiles[last]):
        collapsed[last][t, PAD : PAD + rows[last], :] = stack[last][t, guide_at : guide_at + rows[last], :]
    for level in range(LEVELS - 2, 0, -1):
        a, b = low[level], high[level]
        for t in range(tiles[level + 1]):
            even, odd = row_up(collapsed[level + 1], t, PAD + a // 2, (b - a) // 2)
            joined[0][t, pl.ds(0, (b - a) // 2, stride=2), :] = even
            joined[0][t, pl.ds(1, (b - a) // 2, stride=2), :] = odd
        x = wide([joined[0][t, 0 : b - a, :] for t in range(tiles[level + 1])])
        y = mm(x, up[level][...])
        for t in range(tiles[level]):
            collapsed[level][t, PAD + a : PAD + b, :] = coefficients[level][t] + y[:, lane(t)]
    pairs = [row_up(collapsed[1], t, coarse_at, half) for t in range(tiles[1])]
    x = jnp.concatenate([wide([p[0] for p in pairs]), wide([p[1] for p in pairs])], axis=0)
    fine = mm(x, up[0][...])
    for t in range(own_tiles):
        for p in range(2):
            result[t, pl.ds(p, half, stride=2), :] = (
                gain[0] * total[t, p * half : (p + 1) * half, :]
                + fine[p * half : (p + 1) * half, lane(t)]
            )
        out[:, lane(t)] = result[t, :, :]


def tone(extended, level_gain, block_rows, block_cols):
    rows, cols, tiles = sizes(block_rows, block_cols)
    anchors = np.arange(CHANNELS, dtype=np.float32) / np.float32(CHANNELS - 1)
    down = [
        down_matrix(cols[l], cols[l + 1], tiles[l], tiles[l + 1]) for l in range(LEVELS - 1)
    ]
    up = [up_matrix(cols[1], HALO_COLS // 2, block_cols, tiles[1], block_cols // LANE)] + [
        up_matrix(cols[l + 1], 0, cols[l], tiles[l + 1], tiles[l]) for l in range(1, LEVELS - 1)
    ]

    def f32(*shape):
        return pltpu.VMEM(shape, jnp.float32)

    def padded(count):
        return -(-count // 8) * 8 + 2 * PAD

    scratch = [
        f32(block_cols // LANE, block_rows, LANE),
        f32(tiles[0], rows[0] + 2 * PAD, LANE),
        f32(tiles[1], rows[1] + 2 * PAD, LANE),
        f32(block_cols // LANE, block_rows, LANE),
        f32(block_cols // LANE, block_rows, LANE),
    ]
    scratch += [f32(tiles[l], padded((CHANNELS + 1) * rows[l]), LANE) for l in range(1, LEVELS)]
    scratch += [f32(tiles[1], padded(rows[1]), LANE)]
    scratch += [f32(tiles[l + 1], padded(CHANNELS * rows[l]), LANE) for l in range(1, LEVELS - 1)]
    scratch += [f32(1, 8, LANE)]
    scratch += [f32(tiles[l], padded(CHANNELS * rows[l]), LANE) for l in range(1, LEVELS - 1)]
    scratch += [f32(tiles[l], padded(rows[l]), LANE) for l in range(1, LEVELS)]
    vmem = pl.BlockSpec(memory_space=pltpu.VMEM)
    smem = pl.BlockSpec(memory_space=pltpu.SMEM)
    return pl.pallas_call(
        functools.partial(tone_kernel, rows, tiles, block_rows, block_cols),
        out_shape=jax.ShapeDtypeStruct((block_rows, block_cols), jnp.float32),
        in_specs=[smem, smem] + [vmem] * 11,
        out_specs=vmem,
        scratch_shapes=scratch,
        compiler_params=pltpu.CompilerParams(vmem_limit_bytes=48 * 1024 * 1024),
        name="tone_pyramid",
    )(level_gain, jnp.asarray(anchors), extended, *[jnp.asarray(m, jnp.bfloat16) for m in down + up])


def solution(mesh):
    placed = (P("row", "col"), P())

    def local(luminance, level_gain):
        extended = exchange(("row", "col"), luminance)
        return tone(extended, level_gain, *luminance.shape)

    return jax.shard_map(
        local, mesh=mesh, in_specs=placed, out_specs=P("row", "col"), check_vma=False
    )
```

```python
import functools
import jax
import jax.numpy as jnp
import numpy as np
from jax import lax
from jax.experimental import pallas as pl
from jax.experimental.pallas import tpu as pltpu
from jax.sharding import PartitionSpec as P

CHANNELS = 16
STACK = CHANNELS + 1
HALO = 32
PAD = 8
LANE = 128
QUARTER = LANE // 4

exponent_scale = -np.log2(np.e) / (2.0 * 0.025 * 0.025)
MESH = pl.DeviceIdType.MESH
STEPS = [(dr, dc) for dr in (-1, 0, 1) for dc in (-1, 0, 1) if (dr, dc) != (0, 0)]


def ceil_to(count, unit):
    return -(-count // unit) * unit


def down_matrix(cols_in, wrap):
    matrix = np.zeros((ceil_to(cols_in, LANE), ceil_to(cols_in // 2, LANE)), np.float32)
    for j in range(cols_in // 2):
        for s, weight in enumerate((0.0625, 0.25, 0.375, 0.25, 0.0625)):
            source = 2 * j + s - 2
            if wrap:
                source %= cols_in
            if 0 <= source < cols_in:
                matrix[source, j] = weight
    return matrix


def up_matrix(fine, place):
    taps = []
    for lane_out, f in enumerate(fine):
        m = f // 2
        weights = ((m - 1, 0.125), (m, 0.75), (m + 1, 0.125)) if f % 2 == 0 else ((m, 0.5), (m + 1, 0.5))
        taps += [(place(source), lane_out, weight) for source, weight in weights]
    taps = [tap for tap in taps if tap[0] is not None]
    matrix = np.zeros((ceil_to(max(t[0] for t in taps) + 1, LANE), ceil_to(len(fine), LANE)), np.float32)
    for source, lane_out, weight in taps:
        matrix[source, lane_out] = weight
    return matrix


def circle(block, level):
    own, side = block >> level, (LANE // 2) >> level
    return list(range(own + side)) + list(range(-side, 0))


def matrices(block_cols):
    def around(level):
        where = {c: i for i, c in enumerate(circle(block_cols, level))}
        return where.get

    def linear(first, count):
        return lambda c: c - first if 0 <= c - first < count else None

    own4 = block_cols >> 4
    down = [down_matrix(len(circle(block_cols, l)), True) for l in range(4)] + [down_matrix(3 * own4, False)]
    up = [up_matrix(list(range(block_cols)), around(1))]
    up += [up_matrix(circle(block_cols, l), around(l + 1)) for l in (1, 2)]
    up += [up_matrix(circle(block_cols, 3), linear(-own4, 3 * own4))]
    up += [up_matrix(list(range(-own4, 2 * own4)), linear(-own4 // 2, 3 * own4 // 2))]
    return down, up


def mm(x, matrix, parts=2):
    total = None
    for part in range(parts):
        head = x.astype(jnp.bfloat16)
        if part < parts - 1:
            x = x - head.astype(jnp.float32)
        term = jnp.dot(head, matrix, preferred_element_type=jnp.float32)
        total = term if total is None else total + term
    return total


def bump(values, anchor):
    offset = values - anchor
    return offset * jnp.exp2(offset * offset * exponent_scale)


def hat(guidance, anchor):
    return jnp.maximum(0.0, 1.0 - jnp.abs(guidance - anchor) * (CHANNELS - 1))


def wide(parts):
    return parts[0] if len(parts) == 1 else jnp.concatenate(parts, axis=1)


def lane(t):
    return slice(t * LANE, (t + 1) * LANE)


def row_down(ref, t, start, count):
    def tap(s):
        return ref[t, pl.ds(start + s - 2, count, stride=2), :]

    return 0.375 * tap(2) + 0.25 * (tap(1) + tap(3)) + 0.0625 * (tap(0) + tap(4))


def row_up(ref, t, start, count):
    before = ref[t, pl.ds(start - 1, count), :]
    here = ref[t, pl.ds(start, count), :]
    after = ref[t, pl.ds(start + 1, count), :]
    return (before + 6.0 * here + after) * 0.125, (here + after) * 0.5


def turn(x, shift):
    shift %= LANE
    return x if shift == 0 else pltpu.roll(x, shift, 1)


def lanes_of(x):
    return lax.broadcasted_iota(jnp.int32, x.shape, 1)


def pack(x, first):
    count = x.shape[0] // 4
    groups = [turn(x[g * count : (g + 1) * count, :], g * QUARTER - first) for g in range(4)]
    return beside(groups)


def beside(groups):
    result = groups[-1]
    index = lanes_of(result)
    for g in reversed(range(len(groups) - 1)):
        result = jnp.where(index < (g + 1) * QUARTER, groups[g], result)
    return result


def chunk_of(count):
    for size in range(320, 0, -8):
        if count % size == 0:
            return size
    return count


def kernel(axes, spans, gain, anchors, lum, bank, out, *refs):
    (top, bottom, side_out, side_in, halo, center, remapped, first, total, result, mats) = refs[:11]
    (g1, g2, g3, g4, e4, g5, u1, u2, u3, u4, v1, v2, v3, v4, c1, c2, c3, c4, c5, packed, gathered) = refs[11:32]
    send_a, recv_a, send_b, recv_b, bank_sem = refs[32:]
    block_rows, block_cols = lum.shape
    own_tiles = block_cols // LANE
    half = block_rows // 2
    counts = [lax.axis_size(a) for a in axes]
    place = [lax.axis_index(a) for a in axes]

    def device(dr, dc):
        return tuple(lax.rem(p + d + n, n) for p, d, n in zip(place, (dr, dc), counts))

    def matrix(name):
        start, depth, width = spans[name]
        return mats[start : start + depth, 0:width]

    bank_copy = pltpu.make_async_copy(bank, mats, bank_sem)
    bank_copy.start()
    barrier = pltpu.get_barrier_semaphore()
    for dr, dc in STEPS:
        pl.semaphore_signal(barrier, inc=1, device_id=device(dr, dc), device_id_type=MESH)

    mid, corner = block_rows // 4, HALO // 4
    for s, (t, start) in enumerate(((0, 0), (own_tiles - 1, LANE - QUARTER))):
        side_out[s, 0:mid, :] = pack(lum[:, lane(t)], start)
        side_out[s, mid : mid + corner, :] = pack(lum[0:HALO, lane(t)], start)
        side_out[s, mid + corner : mid + 2 * corner, :] = pack(lum[block_rows - HALO :, lane(t)], start)
    for t in range(own_tiles):
        center[t, :, :] = lum[:, lane(t)]
    total[...] = jnp.zeros_like(total)
    pl.semaphore_wait(barrier, len(STEPS))

    rows_at = {0: (0, mid), -1: (mid, corner), 1: (mid + corner, corner)}
    copies = []
    for index, (dr, dc) in enumerate(STEPS):
        if dc == 0:
            src = lum.at[pl.ds(0 if dr < 0 else block_rows - HALO, HALO), :]
            dst = bottom if dr < 0 else top
        else:
            s = 0 if dc < 0 else 1
            src = side_out.at[s, pl.ds(*rows_at[dr]), :]
            dst = side_in.at[1 - s, pl.ds(*rows_at[-dr]), :]
        copy = pltpu.make_async_remote_copy(
            src_ref=src,
            dst_ref=dst,
            send_sem=send_a.at[index],
            recv_sem=recv_a.at[index],
            device_id=device(dr, dc),
            device_id_type=MESH,
        )
        copy.start()
        copies.append(copy)
    for copy in copies:
        copy.wait()
    bank_copy.wait()

    ext_rows = block_rows + 2 * HALO
    for start, (at, count) in ((0, rows_at[-1]), (HALO, rows_at[0]), (HALO + block_rows, rows_at[1])):
        left, right = side_in[0, at : at + count, :], side_in[1, at : at + count, :]
        index = lanes_of(left)
        for g in range(4):
            halo[start + g * count : start + (g + 1) * count, :] = jnp.where(
                index < LANE // 2, turn(right, -g * QUARTER), turn(left, LANE - QUARTER - g * QUARTER)
            )

    def extended(t):
        if t == own_tiles:
            return [(r, halo[r : r + 64, :]) for r in range(0, ext_rows, 64)]
        inner = [(HALO + r, lum[r : r + 64, lane(t)]) for r in range(0, block_rows, 64)]
        return [(0, top[:, lane(t)])] + inner + [(HALO + block_rows, bottom[:, lane(t)])]

    rows1 = ext_rows // 2
    tiles1 = first.shape[0]
    coarse_at = PAD + HALO // 2

    def finest(dst_row, prepare, weigh):
        for t in range(own_tiles + 1):
            for r, values in extended(t):
                remapped[t, PAD + r : PAD + r + values.shape[0], :] = prepare(values)
        x = wide([row_down(remapped, t, PAD, rows1) for t in range(own_tiles + 1)])
        y = mm(x, matrix("d0"))
        for t in range(tiles1):
            g1[t, pl.ds(dst_row, rows1), :] = y[:, lane(t)]
            first[t, PAD : PAD + rows1, :] = y[:, lane(t)]
        pairs = [row_up(first, t, coarse_at, half) for t in range(tiles1)]
        x = jnp.concatenate([wide([p[0] for p in pairs]), wide([p[1] for p in pairs])], axis=0)
        fine = mm(x, matrix("u0"))
        for t in range(own_tiles):
            for p in range(2):
                value = remapped[t, pl.ds(PAD + HALO + p, half, stride=2), :]
                total[t, p * half : (p + 1) * half, :] += weigh(t, p) * (
                    value - fine[p * half : (p + 1) * half, lane(t)]
                )

    def channel(k, carry):
        anchor = anchors[k]
        finest(
            pl.multiple_of(PAD + k * rows1, 8),
            lambda values: bump(values, anchor),
            lambda t, p: hat(center[t, pl.ds(p, half, stride=2), :], anchor),
        )
        return carry

    lax.fori_loop(0, CHANNELS, channel, 0)
    finest(PAD + CHANNELS * rows1, lambda values: values, lambda t, p: 0.5)

    def shrink(src, dst, name, count):
        step = chunk_of(count)
        for o in range(0, count, step):
            x = wide([row_down(src, t, PAD + 2 * o, step) for t in range(src.shape[0])])
            y = mm(x, matrix(name))
            for t in range(dst.shape[0]):
                dst[t, PAD + o : PAD + o + step, :] = y[:, lane(t)]

    rows2, rows3, rows4 = rows1 // 2, rows1 // 4, rows1 // 8
    shrink(g1, g2, "d1", STACK * rows2)
    shrink(g2, g3, "d2", STACK * rows3)
    shrink(g3, g4, "d3", STACK * rows4)

    own4 = block_rows // 16
    skip4 = HALO // 16
    groups = -(-STACK // 4)
    for g in range(groups):
        members = []
        for q in range(4):
            k = min(4 * g + q, CHANNELS)
            at = PAD + k * rows4 + skip4
            members.append(turn(g4[0, at : at + own4, :], q * QUARTER))
        packed[g * own4 : (g + 1) * own4, :] = beside(members)
    copies = []
    for index, (dr, dc) in enumerate(STEPS):
        copy = pltpu.make_async_remote_copy(
            src_ref=packed,
            dst_ref=gathered.at[len(STEPS) - 1 - index],
            send_sem=send_b.at[index],
            recv_sem=recv_b.at[index],
            device_id=device(dr, dc),
            device_id_type=MESH,
        )
        copy.start()
        copies.append(copy)

    def detail(level, fine_stack, coarse_stack, spread, wider, name, fine, coarse, skip, a, b):
        count = STACK * coarse
        step = chunk_of(count)
        for o in range(0, count, step):
            for t in range(coarse_stack.shape[0]):
                even, odd = row_up(coarse_stack, t, PAD + o, step)
                spread[t, pl.ds(2 * o, step, stride=2), :] = even
                spread[t, pl.ds(2 * o + 1, step, stride=2), :] = odd
            x = wide([spread[t, 2 * o : 2 * (o + step), :] for t in range(coarse_stack.shape[0])])
            y = mm(x, matrix(name))
            for t in range(fine_stack.shape[0]):
                wider[t, 2 * o : 2 * (o + step), :] = y[:, lane(t)]
        sums = []
        for t in range(fine_stack.shape[0]):

            def difference(k):
                at = k * 2 * coarse + skip
                return (
                    fine_stack[t, PAD + k * fine + a : PAD + k * fine + b, :]
                    - wider[t, at + a : at + b, :]
                )

            guidance = fine_stack[t, PAD + CHANNELS * fine + a : PAD + CHANNELS * fine + b, :]
            running = 0.5 * difference(CHANNELS)
            for k in range(CHANNELS):
                anchor = np.float32(k) / np.float32(CHANNELS - 1)
                running = running + hat(guidance, anchor) * difference(k)
            sums.append(gain[level] * running)
        return sums

    near = HALO // 2 - 8
    coef1 = detail(1, g1, g2, u1, v1, "u1", rows1, rows2, 0, near, rows1 - near)
    coef2 = detail(2, g2, g3, u2, v2, "u2", rows2, rows3, 0, 0, rows2)

    for copy in copies:
        copy.wait()
    for k in range(STACK):
        g, q = divmod(k, 4)
        for dr in (-1, 0, 1):
            members = []
            for dc in (-1, 0, 1):
                if (dr, dc) == (0, 0):
                    piece = packed[g * own4 : (g + 1) * own4, :]
                else:
                    piece = gathered[STEPS.index((dr, dc)), g * own4 : (g + 1) * own4, :]
                members.append(turn(piece, (dc + 1 - q) * QUARTER))
            at = PAD + (3 * k + dr + 1) * own4
            e4[0, at : at + own4, :] = beside(members)

    ext4 = 3 * own4
    ext5 = ext4 // 2
    shrink(e4, g5, "d4", STACK * ext5)
    coef3 = detail(3, g3, e4, u3, v3, "u3", rows3, ext4, 2 * (own4 - skip4), 0, rows3)
    coef4 = detail(4, e4, g5, u4, v4, "u4", ext4, ext5, 0, 0, ext4)

    guide_at = PAD + CHANNELS * ext5
    c5[0, PAD : PAD + ext5, :] = g5[0, guide_at : guide_at + ext5, :]

    def collapse(coarse, start, fine, at, coefficients, name):
        count = coefficients[0].shape[0] // 2
        for t in range(coarse.shape[0]):
            even, odd = row_up(coarse, t, PAD + start, count)
            u1[t, pl.ds(0, count, stride=2), :] = even
            u1[t, pl.ds(1, count, stride=2), :] = odd
        y = mm(wide([u1[t, 0 : 2 * count, :] for t in range(coarse.shape[0])]), matrix(name), 3)
        for t in range(fine.shape[0]):
            fine[t, PAD + at : PAD + at + 2 * count, :] = coefficients[t] + y[:, lane(t)]

    collapse(c5, 0, c4, 0, coef4, "u4")
    collapse(c4, own4 - skip4, c3, 0, coef3, "u3")
    collapse(c3, 0, c2, 0, coef2, "u2")
    collapse(c2, near // 2, c1, near, coef1, "u1")
    pairs = [row_up(c1, t, coarse_at, half) for t in range(tiles1)]
    x = jnp.concatenate([wide([p[0] for p in pairs]), wide([p[1] for p in pairs])], axis=0)
    fine = mm(x, matrix("u0"), 3)
    for t in range(own_tiles):
        for p in range(2):
            result[t, pl.ds(p, half, stride=2), :] = (
                gain[0] * total[t, p * half : (p + 1) * half, :]
                + fine[p * half : (p + 1) * half, lane(t)]
            )
        out[:, lane(t)] = result[t, :, :]


def tone(axes, luminance, level_gain):
    block_rows, block_cols = luminance.shape
    anchors = np.arange(CHANNELS, dtype=np.float32) / np.float32(CHANNELS - 1)
    down, up = matrices(block_cols)
    spans, parts, start = {}, [], 0
    width = max(m.shape[1] for m in down + up)
    for prefix, group in (("d", down), ("u", up)):
        for level, m in enumerate(group):
            spans[prefix + str(level)] = (start, *m.shape)
            parts.append(np.pad(m, ((0, 0), (0, width - m.shape[1]))))
            start += m.shape[0]
    bank = jnp.asarray(np.concatenate(parts), jnp.bfloat16)

    def f32(*shape):
        return pltpu.VMEM(shape, jnp.float32)

    def stack(tiles, count):
        return f32(tiles, ceil_to(count, 8) + 2 * PAD, LANE)

    own_tiles = block_cols // LANE
    tiles = [-(-len(circle(block_cols, l)) // LANE) for l in range(4)] + [1, 1]
    ext = block_rows + 2 * HALO
    rows = [ext >> l for l in range(5)]
    own4 = block_rows // 16
    ext4, ext5 = 3 * own4, 3 * own4 // 2
    side = block_rows // 4 + HALO // 2
    scratch = [
        f32(HALO, block_cols),
        f32(HALO, block_cols),
        f32(2, side, LANE),
        f32(2, side, LANE),
        f32(ext, LANE),
        f32(own_tiles, block_rows, LANE),
        stack(own_tiles + 1, ext),
        stack(tiles[1], rows[1]),
        f32(own_tiles, block_rows, LANE),
        f32(own_tiles, block_rows, LANE),
        pltpu.VMEM(bank.shape, jnp.bfloat16),
        stack(tiles[1], STACK * rows[1]),
        stack(tiles[2], STACK * rows[2]),
        stack(tiles[3], STACK * rows[3]),
        stack(1, STACK * rows[4]),
        stack(1, STACK * ext4),
        stack(1, STACK * ext5),
        stack(tiles[2], STACK * rows[1]),
        stack(tiles[3], STACK * rows[2]),
        stack(1, STACK * 2 * ext4),
        stack(1, STACK * ext4),
        stack(tiles[1], STACK * rows[1]),
        stack(tiles[2], STACK * rows[2]),
        stack(tiles[3], STACK * 2 * ext4),
        stack(1, STACK * ext4),
        stack(tiles[1], rows[1]),
        stack(tiles[2], rows[2]),
        stack(tiles[3], rows[3]),
        stack(1, ext4),
        stack(1, ext5),
        f32(-(-STACK // 4) * own4, LANE),
        f32(len(STEPS), -(-STACK // 4) * own4, LANE),
    ]
    dma = pltpu.SemaphoreType.DMA
    scratch += [dma((8,)), dma((8,)), dma((8,)), dma((8,)), dma]
    vmem = pl.BlockSpec(memory_space=pltpu.VMEM)
    smem = pl.BlockSpec(memory_space=pltpu.SMEM)
    return pl.pallas_call(
        functools.partial(kernel, axes, spans),
        out_shape=jax.ShapeDtypeStruct((block_rows, block_cols), jnp.float32),
        in_specs=[smem, smem, vmem, pl.BlockSpec(memory_space=pl.ANY)],
        out_specs=vmem,
        scratch_shapes=scratch,
        compiler_params=pltpu.CompilerParams(
            vmem_limit_bytes=48 * 1024 * 1024, collective_id=0, has_side_effects=True
        ),
        name="tone_pyramid",
    )(level_gain, jnp.asarray(anchors), luminance, bank)


def solution(mesh):
    placed = (P("row", "col"), P())

    def local(luminance, level_gain):
        return tone(("row", "col"), luminance, level_gain)

    return jax.shard_map(
        local, mesh=mesh, in_specs=placed, out_specs=P("row", "col"), check_vma=False
    )
```

```python
import functools
import jax
import jax.numpy as jnp
import numpy as np
from jax import lax
from jax.experimental import pallas as pl
from jax.experimental.pallas import tpu as pltpu
from jax.sharding import PartitionSpec as P

CHANNELS = 16
STACK = CHANNELS + 1
HALO = 32
PAD = 8
GROUP = 4
LANE = 128
QUARTER = LANE // 4

exponent_scale = -np.log2(np.e) / (2.0 * 0.025 * 0.025)
MESH = pl.DeviceIdType.MESH
STEPS = [(dr, dc) for dr in (-1, 0, 1) for dc in (-1, 0, 1) if (dr, dc) != (0, 0)]


def ceil_to(count, unit):
    return -(-count // unit) * unit


def down_matrix(cols_in, wrap):
    matrix = np.zeros((ceil_to(cols_in, LANE), ceil_to(cols_in // 2, LANE)), np.float32)
    for j in range(cols_in // 2):
        for s, weight in enumerate((0.0625, 0.25, 0.375, 0.25, 0.0625)):
            source = 2 * j + s - 2
            if wrap:
                source %= cols_in
            if 0 <= source < cols_in:
                matrix[source, j] = weight
    return matrix


def up_matrix(fine, place):
    taps = []
    for lane_out, f in enumerate(fine):
        m = f // 2
        weights = ((m - 1, 0.125), (m, 0.75), (m + 1, 0.125)) if f % 2 == 0 else ((m, 0.5), (m + 1, 0.5))
        taps += [(place(source), lane_out, weight) for source, weight in weights]
    taps = [tap for tap in taps if tap[0] is not None]
    matrix = np.zeros((ceil_to(max(t[0] for t in taps) + 1, LANE), ceil_to(len(fine), LANE)), np.float32)
    for source, lane_out, weight in taps:
        matrix[source, lane_out] = weight
    return matrix


def circle(block, level):
    own, side = block >> level, (LANE // 2) >> level
    return list(range(own + side)) + list(range(-side, 0))


def matrices(block_cols):
    def around(level):
        where = {c: i for i, c in enumerate(circle(block_cols, level))}
        return where.get

    def linear(first, count):
        return lambda c: c - first if 0 <= c - first < count else None

    own4 = block_cols >> 4
    down = [down_matrix(len(circle(block_cols, l)), True) for l in range(4)] + [down_matrix(3 * own4, False)]
    up = [up_matrix(list(range(block_cols)), around(1))]
    up += [up_matrix(circle(block_cols, l), around(l + 1)) for l in (1, 2)]
    up += [up_matrix(circle(block_cols, 3), linear(-own4, 3 * own4))]
    up += [up_matrix(list(range(-own4, 2 * own4)), linear(-own4 // 2, 3 * own4 // 2))]
    return down, up


def mm(x, matrix, parts=2):
    heads = []
    for part in range(parts):
        heads.append(x.astype(jnp.bfloat16))
        if part < parts - 1:
            x = x - heads[-1].astype(jnp.float32)
    total = jnp.dot(wide(heads[:2]), matrix, preferred_element_type=jnp.float32)
    if parts == 3:
        total += jnp.dot(heads[2], matrix[: x.shape[1], :], preferred_element_type=jnp.float32)
    return total


def bump(values, anchor):
    offset = values - anchor
    return offset * jnp.exp2(offset * offset * exponent_scale)


def hat(guidance, anchor):
    return jnp.maximum(0.0, 1.0 - jnp.abs(guidance - anchor) * (CHANNELS - 1))


def anchor_of(k):
    return np.float32(k) / np.float32(CHANNELS - 1)


def wide(parts):
    return parts[0] if len(parts) == 1 else jnp.concatenate(parts, axis=1)


def lane(t):
    return slice(t * LANE, (t + 1) * LANE)


def row_down(ref, lead, start, count):
    lead = lead if isinstance(lead, tuple) else (lead,)

    def tap(s):
        return ref[(*lead, pl.ds(start + s - 2, count, stride=2), slice(None))]

    return 0.375 * tap(2) + 0.25 * (tap(1) + tap(3)) + 0.0625 * (tap(0) + tap(4))


def row_up(ref, t, start, count):
    before = ref[t, pl.ds(start - 1, count), :]
    here = ref[t, pl.ds(start, count), :]
    after = ref[t, pl.ds(start + 1, count), :]
    return (before + 6.0 * here + after) * 0.125, (here + after) * 0.5


def turn(x, shift):
    shift %= LANE
    return x if shift == 0 else pltpu.roll(x, shift, 1)


def lanes_of(x):
    return lax.broadcasted_iota(jnp.int32, x.shape, 1)


def pack(x, first):
    count = x.shape[0] // 4
    groups = [turn(x[g * count : (g + 1) * count, :], g * QUARTER - first) for g in range(4)]
    return beside(groups)


def beside(groups):
    result = groups[-1]
    index = lanes_of(result)
    for g in reversed(range(len(groups) - 1)):
        result = jnp.where(index < (g + 1) * QUARTER, groups[g], result)
    return result


def chunk_of(count):
    for size in range(320, 0, -8):
        if count % size == 0:
            return size
    return count


def kernel(axes, spans, gain_hbm, lum_hbm, bank, out, *refs):
    (gain, lum, top, bottom, side_out, side_in, halo, center, remapped, weights, first, total, result, mats) = refs[:14]
    (g1, g2, g3, g4, e4, g5, u1, u2, u3, u4, v1, v2, v3, v4, c1, c2, c3, c4, c5, packed, gathered) = refs[14:35]
    send_a, recv_a, send_b, recv_b, bank_sem, lum_sem, gain_sem = refs[35:]
    block_rows, block_cols = lum.shape
    own_tiles = block_cols // LANE
    half = block_rows // 2
    counts = [lax.axis_size(a) for a in axes]
    place = [lax.axis_index(a) for a in axes]

    def device(dr, dc):
        return tuple(lax.rem(p + d + n, n) for p, d, n in zip(place, (dr, dc), counts))

    def matrix(name):
        start, depth, count = spans[name]
        whole = wide([mats[start + t * depth : start + (t + 1) * depth, :] for t in range(count)])
        return jnp.concatenate([whole, whole], axis=0)

    barrier = pltpu.get_barrier_semaphore()
    for dr, dc in STEPS:
        pl.semaphore_signal(barrier, inc=1, device_id=device(dr, dc), device_id_type=MESH)
    lum_copy = pltpu.make_async_copy(lum_hbm, lum, lum_sem)
    lum_copy.start()
    gain_copy = pltpu.make_async_copy(gain_hbm, gain, gain_sem)
    gain_copy.start()
    bank_copy = pltpu.make_async_copy(bank, mats, bank_sem)
    bank_copy.start()
    lum_copy.wait()

    mid, corner = block_rows // 4, HALO // 4
    for s, (t, start) in enumerate(((0, 0), (own_tiles - 1, LANE - QUARTER))):
        side_out[s, 0:mid, :] = pack(lum[:, lane(t)], start)
        side_out[s, mid : mid + corner, :] = pack(lum[0:HALO, lane(t)], start)
        side_out[s, mid + corner : mid + 2 * corner, :] = pack(lum[block_rows - HALO :, lane(t)], start)
    pl.semaphore_wait(barrier, len(STEPS))

    rows_at = {0: (0, mid), -1: (mid, corner), 1: (mid + corner, corner)}
    copies = []
    for index, (dr, dc) in enumerate(STEPS):
        if dc == 0:
            src = lum.at[pl.ds(0 if dr < 0 else block_rows - HALO, HALO), :]
            dst = bottom if dr < 0 else top
        else:
            s = 0 if dc < 0 else 1
            src = side_out.at[s, pl.ds(*rows_at[dr]), :]
            dst = side_in.at[1 - s, pl.ds(*rows_at[-dr]), :]
        copy = pltpu.make_async_remote_copy(
            src_ref=src,
            dst_ref=dst,
            send_sem=send_a.at[index],
            recv_sem=recv_a.at[index],
            device_id=device(dr, dc),
            device_id_type=MESH,
        )
        copy.start()
        copies.append(copy)
    for t in range(own_tiles):
        center[t, :, :] = lum[:, lane(t)]
    total[...] = jnp.zeros_like(total)

    def own_cells(t, carry):
        for r in range(0, block_rows, 32):
            values = center[t, r : r + 32, :]
            remapped[CHANNELS, t, PAD + HALO + r : PAD + HALO + r + 32, :] = values
            running = 0.5 * values
            for k in range(CHANNELS):
                value, weight = bump(values, anchor_of(k)), hat(values, anchor_of(k))
                remapped[k, t, PAD + HALO + r : PAD + HALO + r + 32, :] = value
                weights[k, t, r : r + 32, :] = weight
                running = running + weight * value
            result[t, r : r + 32, :] = running
        return carry

    lax.fori_loop(0, own_tiles, own_cells, 0)
    for copy in copies:
        copy.wait()
    bank_copy.wait()
    gain_copy.wait()

    ext_rows = block_rows + 2 * HALO
    for start, (at, count) in ((0, rows_at[-1]), (HALO, rows_at[0]), (HALO + block_rows, rows_at[1])):
        left, right = side_in[0, at : at + count, :], side_in[1, at : at + count, :]
        index = lanes_of(left)
        for g in range(4):
            halo[start + g * count : start + (g + 1) * count, :] = jnp.where(
                index < LANE // 2, turn(right, -g * QUARTER), turn(left, LANE - QUARTER - g * QUARTER)
            )

    def beyond(t):
        if t == own_tiles:
            return [(r, halo[r : r + 64, :]) for r in range(0, ext_rows, 64)]
        return [(0, top[:, lane(t)]), (HALO + block_rows, bottom[:, lane(t)])]

    rows1 = ext_rows // 2
    tiles1 = first.shape[0]
    coarse_at = PAD + HALO // 2

    def finest(members, dst_row, prepare, weigh):
        for k in members:
            for t in range(own_tiles + 1):
                for r, values in beyond(t):
                    remapped[k, t, PAD + r : PAD + r + values.shape[0], :] = prepare(values, k)
        x = [
            wide([row_down(remapped, (k, t), PAD, rows1) for t in range(own_tiles + 1)])
            for k in members
        ]
        y = mm(jnp.concatenate(x, axis=0), matrix("d0"))
        count = len(members) * rows1
        for t in range(tiles1):
            g1[t, pl.ds(dst_row, count), :] = y[:, lane(t)]
            first[t, PAD : PAD + count, :] = y[:, lane(t)]
        x = []
        for q in range(len(members)):
            pairs = [row_up(first, t, coarse_at + q * rows1, half) for t in range(tiles1)]
            x += [wide([p[0] for p in pairs]), wide([p[1] for p in pairs])]
        fine = mm(jnp.concatenate(x, axis=0), matrix("u0"))
        for t in range(own_tiles):
            for p in range(2):
                running = total[t, p * half : (p + 1) * half, :]
                for q, k in enumerate(members):
                    at = (2 * q + p) * half
                    running = running + weigh(k, t, p) * fine[at : at + half, lane(t)]
                total[t, p * half : (p + 1) * half, :] = running

    def channels(j, carry):
        finest(
            [GROUP * j + q for q in range(GROUP)],
            pl.multiple_of(PAD + GROUP * j * rows1, 8),
            lambda values, k: bump(values, k.astype(jnp.float32) * np.float32(1.0 / (CHANNELS - 1))),
            lambda k, t, p: weights[k, t, pl.ds(p, half, stride=2), :],
        )
        return carry

    lax.fori_loop(0, CHANNELS // GROUP, channels, 0)
    finest([CHANNELS], PAD + CHANNELS * rows1, lambda values, k: values, lambda k, t, p: 0.5)

    def shrink(src, dst, name, count):
        step = chunk_of(count)
        for o in range(0, count, step):
            x = wide([row_down(src, t, PAD + 2 * o, step) for t in range(src.shape[0])])
            y = mm(x, matrix(name))
            for t in range(dst.shape[0]):
                dst[t, PAD + o : PAD + o + step, :] = y[:, lane(t)]

    rows2, rows3, rows4 = rows1 // 2, rows1 // 4, rows1 // 8
    shrink(g1, g2, "d1", STACK * rows2)
    shrink(g2, g3, "d2", STACK * rows3)
    shrink(g3, g4, "d3", STACK * rows4)

    own4 = block_rows // 16
    skip4 = HALO // 16
    groups = -(-STACK // 4)
    for g in range(groups):
        members = []
        for q in range(4):
            k = min(4 * g + q, CHANNELS)
            at = PAD + k * rows4 + skip4
            members.append(turn(g4[0, at : at + own4, :], q * QUARTER))
        packed[g * own4 : (g + 1) * own4, :] = beside(members)
    copies = []
    for index, (dr, dc) in enumerate(STEPS):
        copy = pltpu.make_async_remote_copy(
            src_ref=packed,
            dst_ref=gathered.at[len(STEPS) - 1 - index],
            send_sem=send_b.at[index],
            recv_sem=recv_b.at[index],
            device_id=device(dr, dc),
            device_id_type=MESH,
        )
        copy.start()
        copies.append(copy)

    def detail(level, fine_stack, coarse_stack, spread, wider, name, fine, coarse, skip, a, b):
        count = STACK * coarse
        step = chunk_of(count)
        for o in range(0, count, step):
            for t in range(coarse_stack.shape[0]):
                even, odd = row_up(coarse_stack, t, PAD + o, step)
                spread[t, pl.ds(2 * o, step, stride=2), :] = even
                spread[t, pl.ds(2 * o + 1, step, stride=2), :] = odd
            x = wide([spread[t, 2 * o : 2 * (o + step), :] for t in range(coarse_stack.shape[0])])
            y = mm(x, matrix(name))
            for t in range(fine_stack.shape[0]):
                wider[t, 2 * o : 2 * (o + step), :] = y[:, lane(t)]
        sums = []
        for t in range(fine_stack.shape[0]):

            def difference(k):
                at = k * 2 * coarse + skip
                return (
                    fine_stack[t, PAD + k * fine + a : PAD + k * fine + b, :]
                    - wider[t, at + a : at + b, :]
                )

            guidance = fine_stack[t, PAD + CHANNELS * fine + a : PAD + CHANNELS * fine + b, :]
            running = 0.5 * difference(CHANNELS)
            for k in range(CHANNELS):
                running = running + hat(guidance, anchor_of(k)) * difference(k)
            sums.append(gain[level] * running)
        return sums

    near = HALO // 2 - 8
    coef1 = detail(1, g1, g2, u1, v1, "u1", rows1, rows2, 0, near, rows1 - near)
    coef2 = detail(2, g2, g3, u2, v2, "u2", rows2, rows3, 0, 0, rows2)

    for copy in copies:
        copy.wait()
    for k in range(STACK):
        g, q = divmod(k, 4)
        for dr in (-1, 0, 1):
            members = []
            for dc in (-1, 0, 1):
                if (dr, dc) == (0, 0):
                    piece = packed[g * own4 : (g + 1) * own4, :]
                else:
                    piece = gathered[STEPS.index((dr, dc)), g * own4 : (g + 1) * own4, :]
                members.append(turn(piece, (dc + 1 - q) * QUARTER))
            at = PAD + (3 * k + dr + 1) * own4
            e4[0, at : at + own4, :] = beside(members)

    ext4 = 3 * own4
    ext5 = ext4 // 2
    shrink(e4, g5, "d4", STACK * ext5)
    coef3 = detail(3, g3, e4, u3, v3, "u3", rows3, ext4, 2 * (own4 - skip4), 0, rows3)
    coef4 = detail(4, e4, g5, u4, v4, "u4", ext4, ext5, 0, 0, ext4)

    guide_at = PAD + CHANNELS * ext5
    c5[0, PAD : PAD + ext5, :] = g5[0, guide_at : guide_at + ext5, :]

    def collapse(coarse, start, fine, at, coefficients, name):
        count = coefficients[0].shape[0] // 2
        for t in range(coarse.shape[0]):
            even, odd = row_up(coarse, t, PAD + start, count)
            u1[t, pl.ds(0, count, stride=2), :] = even
            u1[t, pl.ds(1, count, stride=2), :] = odd
        y = mm(wide([u1[t, 0 : 2 * count, :] for t in range(coarse.shape[0])]), matrix(name), 3)
        for t in range(fine.shape[0]):
            fine[t, PAD + at : PAD + at + 2 * count, :] = coefficients[t] + y[:, lane(t)]

    collapse(c5, 0, c4, 0, coef4, "u4")
    collapse(c4, own4 - skip4, c3, 0, coef3, "u3")
    collapse(c3, 0, c2, 0, coef2, "u2")
    collapse(c2, near // 2, c1, near, coef1, "u1")
    pairs = [row_up(c1, t, coarse_at, half) for t in range(tiles1)]
    x = jnp.concatenate([wide([p[0] for p in pairs]), wide([p[1] for p in pairs])], axis=0)
    fine = mm(x, matrix("u0"), 3)
    for t in range(own_tiles):
        for p in range(2):
            own = result[t, pl.ds(p, half, stride=2), :] - total[t, p * half : (p + 1) * half, :]
            result[t, pl.ds(p, half, stride=2), :] = (
                gain[0] * own + fine[p * half : (p + 1) * half, lane(t)]
            )
        out[:, lane(t)] = result[t, :, :]


def tone(axes, luminance, level_gain):
    block_rows, block_cols = luminance.shape
    down, up = matrices(block_cols)
    spans, parts, start = {}, [], 0
    for prefix, group in (("d", down), ("u", up)):
        for level, m in enumerate(group):
            count = m.shape[1] // LANE
            spans[prefix + str(level)] = (start, m.shape[0], count)
            parts += [m[:, lane(t)] for t in range(count)]
            start += m.shape[0] * count
    bank = jnp.asarray(np.concatenate(parts), jnp.bfloat16)

    def f32(*shape):
        return pltpu.VMEM(shape, jnp.float32)

    def stack(tiles, count):
        return f32(tiles, ceil_to(count, 8) + 2 * PAD, LANE)

    own_tiles = block_cols // LANE
    tiles = [-(-len(circle(block_cols, l)) // LANE) for l in range(4)] + [1, 1]
    ext = block_rows + 2 * HALO
    rows = [ext >> l for l in range(5)]
    own4 = block_rows // 16
    ext4, ext5 = 3 * own4, 3 * own4 // 2
    side = block_rows // 4 + HALO // 2
    scratch = [
        pltpu.SMEM(level_gain.shape, jnp.float32),
        f32(block_rows, block_cols),
        f32(HALO, block_cols),
        f32(HALO, block_cols),
        f32(2, side, LANE),
        f32(2, side, LANE),
        f32(ext, LANE),
        f32(own_tiles, block_rows, LANE),
        f32(STACK, own_tiles + 1, ext + 2 * PAD, LANE),
        f32(CHANNELS, own_tiles, block_rows, LANE),
        stack(tiles[1], GROUP * rows[1]),
        f32(own_tiles, block_rows, LANE),
        f32(own_tiles, block_rows, LANE),
        pltpu.VMEM(bank.shape, jnp.bfloat16),
        stack(tiles[1], STACK * rows[1]),
        stack(tiles[2], STACK * rows[2]),
        stack(tiles[3], STACK * rows[3]),
        stack(1, STACK * rows[4]),
        stack(1, STACK * ext4),
        stack(1, STACK * ext5),
        stack(tiles[2], STACK * rows[1]),
        stack(tiles[3], STACK * rows[2]),
        stack(1, STACK * 2 * ext4),
        stack(1, STACK * ext4),
        stack(tiles[1], STACK * rows[1]),
        stack(tiles[2], STACK * rows[2]),
        stack(tiles[3], STACK * 2 * ext4),
        stack(1, STACK * ext4),
        stack(tiles[1], rows[1]),
        stack(tiles[2], rows[2]),
        stack(tiles[3], rows[3]),
        stack(1, ext4),
        stack(1, ext5),
        f32(-(-STACK // 4) * own4, LANE),
        f32(len(STEPS), -(-STACK // 4) * own4, LANE),
    ]
    dma = pltpu.SemaphoreType.DMA
    scratch += [dma((8,)), dma((8,)), dma((8,)), dma((8,)), dma, dma, dma]
    vmem = pl.BlockSpec(memory_space=pltpu.VMEM)
    hbm = pl.BlockSpec(memory_space=pltpu.HBM)
    return pl.pallas_call(
        functools.partial(kernel, axes, spans),
        out_shape=jax.ShapeDtypeStruct((block_rows, block_cols), jnp.float32),
        in_specs=[hbm, hbm, hbm],
        out_specs=vmem,
        scratch_shapes=scratch,
        compiler_params=pltpu.CompilerParams(
            vmem_limit_bytes=56 * 1024 * 1024, collective_id=0, has_side_effects=True
        ),
        name="tone_pyramid",
    )(level_gain, luminance, bank)


def solution(mesh):
    placed = (P("row", "col"), P())

    def local(luminance, level_gain):
        return tone(("row", "col"), luminance, level_gain)

    return jax.shard_map(
        local, mesh=mesh, in_specs=placed, out_specs=P("row", "col"), check_vma=False
    )
```

```python
import functools
import jax
import jax.numpy as jnp
import numpy as np
from jax import lax
from jax.experimental import pallas as pl
from jax.experimental.pallas import tpu as pltpu
from jax.sharding import PartitionSpec as P

CHANNELS = 16
STACK = CHANNELS + 1
HALO = 32
PAD = 8
GROUP = 8
LANE = 128
QUARTER = LANE // 4

exponent_scale = -np.log2(np.e) / (2.0 * 0.025 * 0.025)
MESH = pl.DeviceIdType.MESH
STEPS = [(dr, dc) for dr in (-1, 0, 1) for dc in (-1, 0, 1) if (dr, dc) != (0, 0)]


def ceil_to(count, unit):
    return -(-count // unit) * unit


def down_matrix(cols_in, wrap):
    matrix = np.zeros((ceil_to(cols_in, LANE), ceil_to(cols_in // 2, LANE)), np.float32)
    for j in range(cols_in // 2):
        for s, weight in enumerate((0.0625, 0.25, 0.375, 0.25, 0.0625)):
            source = 2 * j + s - 2
            if wrap:
                source %= cols_in
            if 0 <= source < cols_in:
                matrix[source, j] = weight
    return matrix


def up_matrix(fine, place):
    taps = []
    for lane_out, f in enumerate(fine):
        m = f // 2
        weights = ((m - 1, 0.125), (m, 0.75), (m + 1, 0.125)) if f % 2 == 0 else ((m, 0.5), (m + 1, 0.5))
        taps += [(place(source), lane_out, weight) for source, weight in weights]
    taps = [tap for tap in taps if tap[0] is not None]
    matrix = np.zeros((ceil_to(max(t[0] for t in taps) + 1, LANE), ceil_to(len(fine), LANE)), np.float32)
    for source, lane_out, weight in taps:
        matrix[source, lane_out] = weight
    return matrix


def circle(block, level):
    own, side = block >> level, (LANE // 2) >> level
    return list(range(own + side)) + list(range(-side, 0))


def matrices(block_cols):
    def around(level):
        where = {c: i for i, c in enumerate(circle(block_cols, level))}
        return where.get

    def linear(first, count):
        return lambda c: c - first if 0 <= c - first < count else None

    own4 = block_cols >> 4
    down = [down_matrix(len(circle(block_cols, l)), True) for l in range(4)] + [down_matrix(3 * own4, False)]
    up = [up_matrix(list(range(block_cols)), around(1))]
    up += [up_matrix(circle(block_cols, l), around(l + 1)) for l in (1, 2)]
    up += [up_matrix(circle(block_cols, 3), linear(-own4, 3 * own4))]
    up += [up_matrix(list(range(-own4, 2 * own4)), linear(-own4 // 2, 3 * own4 // 2))]
    return down, up


def mm(x, matrix, parts=2):
    heads = []
    for part in range(parts):
        heads.append(x.astype(jnp.bfloat16))
        if part < parts - 1:
            x = x - heads[-1].astype(jnp.float32)
    total = jnp.dot(wide(heads[:2]), matrix, preferred_element_type=jnp.float32)
    if parts == 3:
        total += jnp.dot(heads[2], matrix[: x.shape[1], :], preferred_element_type=jnp.float32)
    return total


def bump(values, anchor):
    offset = values - anchor
    return offset * jnp.exp2(offset * offset * exponent_scale)


def hat(guidance, anchor):
    return jnp.maximum(0.0, 1.0 - jnp.abs(guidance - anchor) * (CHANNELS - 1))


def anchor_of(k):
    return np.float32(k) / np.float32(CHANNELS - 1)


def wide(parts):
    return parts[0] if len(parts) == 1 else jnp.concatenate(parts, axis=1)


def lane(t):
    return slice(t * LANE, (t + 1) * LANE)


def row_down(ref, lead, start, count):
    lead = lead if isinstance(lead, tuple) else (lead,)

    def tap(s):
        return ref[(*lead, pl.ds(start + s - 2, count, stride=2), slice(None))]

    return 0.375 * tap(2) + 0.25 * (tap(1) + tap(3)) + 0.0625 * (tap(0) + tap(4))


def row_up(ref, t, start, count):
    before = ref[t, pl.ds(start - 1, count), :]
    here = ref[t, pl.ds(start, count), :]
    after = ref[t, pl.ds(start + 1, count), :]
    return (before + 6.0 * here + after) * 0.125, (here + after) * 0.5


def turn(x, shift):
    shift %= LANE
    return x if shift == 0 else pltpu.roll(x, shift, 1)


def lanes_of(x):
    return lax.broadcasted_iota(jnp.int32, x.shape, 1)


def pack(x, first):
    count = x.shape[0] // 4
    groups = [turn(x[g * count : (g + 1) * count, :], g * QUARTER - first) for g in range(4)]
    return beside(groups)


def beside(groups):
    result = groups[-1]
    index = lanes_of(result)
    for g in reversed(range(len(groups) - 1)):
        result = jnp.where(index < (g + 1) * QUARTER, groups[g], result)
    return result


def chunk_of(count):
    for size in range(320, 0, -8):
        if count % size == 0:
            return size
    return count


def kernel(axes, spans, gain_hbm, lum_hbm, bank, out, *refs):
    (gain, lum, top, bottom, side_out, side_in, halo, center, remapped, weights, total, result, mats) = refs[:13]
    (g1, g2, g3, g4, e4, g5, u1, u2, u3, u4, v1, v2, v3, v4, c1, c2, c3, c4, c5, packed, gathered) = refs[13:34]
    send_a, recv_a, send_b, recv_b, bank_sem, lum_sem, gain_sem = refs[34:]
    block_rows, block_cols = lum.shape
    own_tiles = block_cols // LANE
    half = block_rows // 2
    counts = [lax.axis_size(a) for a in axes]
    place = [lax.axis_index(a) for a in axes]

    def device(dr, dc):
        return tuple(lax.rem(p + d + n, n) for p, d, n in zip(place, (dr, dc), counts))

    def matrix(name):
        start, depth, count = spans[name]
        whole = wide([mats[start + t * depth : start + (t + 1) * depth, :] for t in range(count)])
        return jnp.concatenate([whole, whole], axis=0)

    barrier = pltpu.get_barrier_semaphore()
    for dr, dc in STEPS:
        pl.semaphore_signal(barrier, inc=1, device_id=device(dr, dc), device_id_type=MESH)
    lum_copy = pltpu.make_async_copy(lum_hbm, lum, lum_sem)
    lum_copy.start()
    gain_copy = pltpu.make_async_copy(gain_hbm, gain, gain_sem)
    gain_copy.start()
    bank_copy = pltpu.make_async_copy(bank, mats, bank_sem)
    bank_copy.start()
    lum_copy.wait()

    mid, corner = block_rows // 4, HALO // 4
    for s, (t, start) in enumerate(((0, 0), (own_tiles - 1, LANE - QUARTER))):
        side_out[s, 0:mid, :] = pack(lum[:, lane(t)], start)
        side_out[s, mid : mid + corner, :] = pack(lum[0:HALO, lane(t)], start)
        side_out[s, mid + corner : mid + 2 * corner, :] = pack(lum[block_rows - HALO :, lane(t)], start)
    pl.semaphore_wait(barrier, len(STEPS))

    rows_at = {0: (0, mid), -1: (mid, corner), 1: (mid + corner, corner)}
    copies = []
    for index, (dr, dc) in enumerate(STEPS):
        if dc == 0:
            src = lum.at[pl.ds(0 if dr < 0 else block_rows - HALO, HALO), :]
            dst = bottom if dr < 0 else top
        else:
            s = 0 if dc < 0 else 1
            src = side_out.at[s, pl.ds(*rows_at[dr]), :]
            dst = side_in.at[1 - s, pl.ds(*rows_at[-dr]), :]
        copy = pltpu.make_async_remote_copy(
            src_ref=src,
            dst_ref=dst,
            send_sem=send_a.at[index],
            recv_sem=recv_a.at[index],
            device_id=device(dr, dc),
            device_id_type=MESH,
        )
        copy.start()
        copies.append(copy)
    for t in range(own_tiles):
        center[t, :, :] = lum[:, lane(t)]
    total[...] = jnp.zeros_like(total)

    def own_cells(t, carry):
        for r in range(0, block_rows, 32):
            values = center[t, r : r + 32, :]
            remapped[CHANNELS, t, PAD + HALO + r : PAD + HALO + r + 32, :] = values
            running = 0.5 * values
            for k in range(CHANNELS):
                value, weight = bump(values, anchor_of(k)), hat(values, anchor_of(k))
                remapped[k, t, PAD + HALO + r : PAD + HALO + r + 32, :] = value
                weights[k, t, r : r + 32, :] = weight
                running = running + weight * value
            result[t, r : r + 32, :] = running
        return carry

    lax.fori_loop(0, own_tiles, own_cells, 0)
    for copy in copies:
        copy.wait()
    bank_copy.wait()
    gain_copy.wait()

    ext_rows = block_rows + 2 * HALO
    for start, (at, count) in ((0, rows_at[-1]), (HALO, rows_at[0]), (HALO + block_rows, rows_at[1])):
        left, right = side_in[0, at : at + count, :], side_in[1, at : at + count, :]
        index = lanes_of(left)
        for g in range(4):
            halo[start + g * count : start + (g + 1) * count, :] = jnp.where(
                index < LANE // 2, turn(right, -g * QUARTER), turn(left, LANE - QUARTER - g * QUARTER)
            )

    def beyond(t):
        if t == own_tiles:
            return [(r, halo[r : r + 64, :]) for r in range(0, ext_rows, 64)]
        return [(0, top[:, lane(t)]), (HALO + block_rows, bottom[:, lane(t)])]

    rows1 = ext_rows // 2
    tiles1 = g1.shape[0]
    coarse_at = PAD + HALO // 2

    def finest_down(members, dst_row, prepare):
        for k in members:
            for t in range(own_tiles + 1):
                for r, values in beyond(t):
                    remapped[k, t, PAD + r : PAD + r + values.shape[0], :] = prepare(values, k)
        x = [
            wide([row_down(remapped, (k, t), PAD, rows1) for t in range(own_tiles + 1)])
            for k in members
        ]
        y = mm(jnp.concatenate(x, axis=0), matrix("d0"))
        for t in range(tiles1):
            g1[t, pl.ds(dst_row, len(members) * rows1), :] = y[:, lane(t)]

    def channels(j, carry):
        finest_down(
            [GROUP * j + q for q in range(GROUP)],
            pl.multiple_of(PAD + GROUP * j * rows1, 8),
            lambda values, k: bump(values, k.astype(jnp.float32) * np.float32(1.0 / (CHANNELS - 1))),
        )
        return carry

    lax.fori_loop(0, CHANNELS // GROUP, channels, 0)
    finest_down([CHANNELS], PAD + CHANNELS * rows1, lambda values, k: values)

    def finest_up(members):
        x = []
        for k in members:
            pairs = [row_up(g1, t, coarse_at + k * rows1, half) for t in range(tiles1)]
            x += [wide([p[0] for p in pairs]), wide([p[1] for p in pairs])]
        fine = mm(jnp.concatenate(x, axis=0), matrix("u0"))
        for t in range(own_tiles):
            for p in range(2):
                running = total[t, p * half : (p + 1) * half, :]
                for q, k in enumerate(members):
                    at = (2 * q + p) * half
                    weight = 0.5 if k == CHANNELS else weights[k, t, pl.ds(p, half, stride=2), :]
                    running = running + weight * fine[at : at + half, lane(t)]
                total[t, p * half : (p + 1) * half, :] = running

    def shrink(src, dst, name, count):
        step = chunk_of(count)
        for o in range(0, count, step):
            x = wide([row_down(src, t, PAD + 2 * o, step) for t in range(src.shape[0])])
            y = mm(x, matrix(name))
            for t in range(dst.shape[0]):
                dst[t, PAD + o : PAD + o + step, :] = y[:, lane(t)]

    rows2, rows3, rows4 = rows1 // 2, rows1 // 4, rows1 // 8
    shrink(g1, g2, "d1", STACK * rows2)
    shrink(g2, g3, "d2", STACK * rows3)
    shrink(g3, g4, "d3", STACK * rows4)

    own4 = block_rows // 16
    skip4 = HALO // 16
    groups = -(-STACK // 4)
    for g in range(groups):
        members = []
        for q in range(4):
            k = min(4 * g + q, CHANNELS)
            at = PAD + k * rows4 + skip4
            members.append(turn(g4[0, at : at + own4, :], q * QUARTER))
        packed[g * own4 : (g + 1) * own4, :] = beside(members)
    copies = []
    for index, (dr, dc) in enumerate(STEPS):
        copy = pltpu.make_async_remote_copy(
            src_ref=packed,
            dst_ref=gathered.at[len(STEPS) - 1 - index],
            send_sem=send_b.at[index],
            recv_sem=recv_b.at[index],
            device_id=device(dr, dc),
            device_id_type=MESH,
        )
        copy.start()
        copies.append(copy)

    def detail(level, fine_stack, coarse_stack, spread, wider, name, fine, coarse, skip, a, b):
        count = STACK * coarse
        step = chunk_of(count)
        for o in range(0, count, step):
            for t in range(coarse_stack.shape[0]):
                even, odd = row_up(coarse_stack, t, PAD + o, step)
                spread[t, pl.ds(2 * o, step, stride=2), :] = even
                spread[t, pl.ds(2 * o + 1, step, stride=2), :] = odd
            x = wide([spread[t, 2 * o : 2 * (o + step), :] for t in range(coarse_stack.shape[0])])
            y = mm(x, matrix(name))
            for t in range(fine_stack.shape[0]):
                wider[t, 2 * o : 2 * (o + step), :] = y[:, lane(t)]
        sums = []
        for t in range(fine_stack.shape[0]):

            def difference(k):
                at = k * 2 * coarse + skip
                return (
                    fine_stack[t, PAD + k * fine + a : PAD + k * fine + b, :]
                    - wider[t, at + a : at + b, :]
                )

            guidance = fine_stack[t, PAD + CHANNELS * fine + a : PAD + CHANNELS * fine + b, :]
            running = 0.5 * difference(CHANNELS)
            for k in range(CHANNELS):
                running = running + hat(guidance, anchor_of(k)) * difference(k)
            sums.append(gain[level] * running)
        return sums

    for k in range(0, CHANNELS, 4):
        finest_up(list(range(k, STACK if k + 4 == CHANNELS else k + 4)))
    near = HALO // 2 - 8
    coef1 = detail(1, g1, g2, u1, v1, "u1", rows1, rows2, 0, near, rows1 - near)
    coef2 = detail(2, g2, g3, u2, v2, "u2", rows2, rows3, 0, 0, rows2)

    for copy in copies:
        copy.wait()
    for k in range(STACK):
        g, q = divmod(k, 4)
        for dr in (-1, 0, 1):
            members = []
            for dc in (-1, 0, 1):
                if (dr, dc) == (0, 0):
                    piece = packed[g * own4 : (g + 1) * own4, :]
                else:
                    piece = gathered[STEPS.index((dr, dc)), g * own4 : (g + 1) * own4, :]
                members.append(turn(piece, (dc + 1 - q) * QUARTER))
            at = PAD + (3 * k + dr + 1) * own4
            e4[0, at : at + own4, :] = beside(members)

    ext4 = 3 * own4
    ext5 = ext4 // 2
    shrink(e4, g5, "d4", STACK * ext5)
    coef3 = detail(3, g3, e4, u3, v3, "u3", rows3, ext4, 2 * (own4 - skip4), 0, rows3)
    coef4 = detail(4, e4, g5, u4, v4, "u4", ext4, ext5, 0, 0, ext4)

    guide_at = PAD + CHANNELS * ext5
    c5[0, PAD : PAD + ext5, :] = g5[0, guide_at : guide_at + ext5, :]

    def collapse(coarse, start, fine, at, coefficients, name):
        count = coefficients[0].shape[0] // 2
        for t in range(coarse.shape[0]):
            even, odd = row_up(coarse, t, PAD + start, count)
            u1[t, pl.ds(0, count, stride=2), :] = even
            u1[t, pl.ds(1, count, stride=2), :] = odd
        y = mm(wide([u1[t, 0 : 2 * count, :] for t in range(coarse.shape[0])]), matrix(name), 3)
        for t in range(fine.shape[0]):
            fine[t, PAD + at : PAD + at + 2 * count, :] = coefficients[t] + y[:, lane(t)]

    collapse(c5, 0, c4, 0, coef4, "u4")
    collapse(c4, own4 - skip4, c3, 0, coef3, "u3")
    collapse(c3, 0, c2, 0, coef2, "u2")
    collapse(c2, near // 2, c1, near, coef1, "u1")
    pairs = [row_up(c1, t, coarse_at, half) for t in range(tiles1)]
    x = jnp.concatenate([wide([p[0] for p in pairs]), wide([p[1] for p in pairs])], axis=0)
    fine = mm(x, matrix("u0"), 3)
    for t in range(own_tiles):
        for p in range(2):
            own = result[t, pl.ds(p, half, stride=2), :] - total[t, p * half : (p + 1) * half, :]
            result[t, pl.ds(p, half, stride=2), :] = (
                gain[0] * own + fine[p * half : (p + 1) * half, lane(t)]
            )
        out[:, lane(t)] = result[t, :, :]


def tone(axes, luminance, level_gain):
    block_rows, block_cols = luminance.shape
    down, up = matrices(block_cols)
    spans, parts, start = {}, [], 0
    for prefix, group in (("d", down), ("u", up)):
        for level, m in enumerate(group):
            count = m.shape[1] // LANE
            spans[prefix + str(level)] = (start, m.shape[0], count)
            parts += [m[:, lane(t)] for t in range(count)]
            start += m.shape[0] * count
    bank = jnp.asarray(np.concatenate(parts), jnp.bfloat16)

    def f32(*shape):
        return pltpu.VMEM(shape, jnp.float32)

    def stack(tiles, count):
        return f32(tiles, ceil_to(count, 8) + 2 * PAD, LANE)

    own_tiles = block_cols // LANE
    tiles = [-(-len(circle(block_cols, l)) // LANE) for l in range(4)] + [1, 1]
    ext = block_rows + 2 * HALO
    rows = [ext >> l for l in range(5)]
    own4 = block_rows // 16
    ext4, ext5 = 3 * own4, 3 * own4 // 2
    side = block_rows // 4 + HALO // 2
    scratch = [
        pltpu.SMEM(level_gain.shape, jnp.float32),
        f32(block_rows, block_cols),
        f32(HALO, block_cols),
        f32(HALO, block_cols),
        f32(2, side, LANE),
        f32(2, side, LANE),
        f32(ext, LANE),
        f32(own_tiles, block_rows, LANE),
        f32(STACK, own_tiles + 1, ext + 2 * PAD, LANE),
        f32(CHANNELS, own_tiles, block_rows, LANE),
        f32(own_tiles, block_rows, LANE),
        f32(own_tiles, block_rows, LANE),
        pltpu.VMEM(bank.shape, jnp.bfloat16),
        stack(tiles[1], STACK * rows[1]),
        stack(tiles[2], STACK * rows[2]),
        stack(tiles[3], STACK * rows[3]),
        stack(1, STACK * rows[4]),
        stack(1, STACK * ext4),
        stack(1, STACK * ext5),
        stack(tiles[2], STACK * rows[1]),
        stack(tiles[3], STACK * rows[2]),
        stack(1, STACK * 2 * ext4),
        stack(1, STACK * ext4),
        stack(tiles[1], STACK * rows[1]),
        stack(tiles[2], STACK * rows[2]),
        stack(tiles[3], STACK * 2 * ext4),
        stack(1, STACK * ext4),
        stack(tiles[1], rows[1]),
        stack(tiles[2], rows[2]),
        stack(tiles[3], rows[3]),
        stack(1, ext4),
        stack(1, ext5),
        f32(-(-STACK // 4) * own4, LANE),
        f32(len(STEPS), -(-STACK // 4) * own4, LANE),
    ]
    dma = pltpu.SemaphoreType.DMA
    scratch += [dma((8,)), dma((8,)), dma((8,)), dma((8,)), dma, dma, dma]
    vmem = pl.BlockSpec(memory_space=pltpu.VMEM)
    hbm = pl.BlockSpec(memory_space=pltpu.HBM)
    return pl.pallas_call(
        functools.partial(kernel, axes, spans),
        out_shape=jax.ShapeDtypeStruct((block_rows, block_cols), jnp.float32),
        in_specs=[hbm, hbm, hbm],
        out_specs=vmem,
        scratch_shapes=scratch,
        compiler_params=pltpu.CompilerParams(
            vmem_limit_bytes=56 * 1024 * 1024, collective_id=0, has_side_effects=True
        ),
        name="tone_pyramid",
    )(level_gain, luminance, bank)


def solution(mesh):
    placed = (P("row", "col"), P())

    def local(luminance, level_gain):
        return tone(("row", "col"), luminance, level_gain)

    return jax.shard_map(
        local, mesh=mesh, in_specs=placed, out_specs=P("row", "col"), check_vma=False
    )
```

```python
import functools
import jax
import jax.numpy as jnp
import numpy as np
from jax import lax
from jax.experimental import pallas as pl
from jax.experimental.pallas import tpu as pltpu
from jax.sharding import PartitionSpec as P

CHANNELS = 16
STACK = CHANNELS + 1
HALO = 32
PAD = 8
GROUP = 8
LANE = 128
QUARTER = LANE // 4

exponent_scale = -np.log2(np.e) / (2.0 * 0.025 * 0.025)
MESH = pl.DeviceIdType.MESH
STEPS = [(dr, dc) for dr in (-1, 0, 1) for dc in (-1, 0, 1) if (dr, dc) != (0, 0)]


def ceil_to(count, unit):
    return -(-count // unit) * unit


def down_matrix(cols_in, wrap):
    matrix = np.zeros((ceil_to(cols_in, LANE), ceil_to(cols_in // 2, LANE)), np.float32)
    for j in range(cols_in // 2):
        for s, weight in enumerate((0.0625, 0.25, 0.375, 0.25, 0.0625)):
            source = 2 * j + s - 2
            if wrap:
                source %= cols_in
            if 0 <= source < cols_in:
                matrix[source, j] = weight
    return matrix


def up_matrix(fine, place):
    taps = []
    for lane_out, f in enumerate(fine):
        m = f // 2
        weights = ((m - 1, 0.125), (m, 0.75), (m + 1, 0.125)) if f % 2 == 0 else ((m, 0.5), (m + 1, 0.5))
        taps += [(place(source), lane_out, weight) for source, weight in weights]
    taps = [tap for tap in taps if tap[0] is not None]
    matrix = np.zeros((ceil_to(max(t[0] for t in taps) + 1, LANE), ceil_to(len(fine), LANE)), np.float32)
    for source, lane_out, weight in taps:
        matrix[source, lane_out] = weight
    return matrix


def circle(block, level):
    own, side = block >> level, (LANE // 2) >> level
    return list(range(own + side)) + list(range(-side, 0))


def matrices(block_cols):
    def around(level):
        where = {c: i for i, c in enumerate(circle(block_cols, level))}
        return where.get

    def linear(first, count):
        return lambda c: c - first if 0 <= c - first < count else None

    own4 = block_cols >> 4
    down = [down_matrix(len(circle(block_cols, l)), True) for l in range(4)] + [down_matrix(3 * own4, False)]
    up = [up_matrix(list(range(block_cols)), around(1))]
    up += [up_matrix(circle(block_cols, l), around(l + 1)) for l in (1, 2)]
    up += [up_matrix(circle(block_cols, 3), linear(-own4, 3 * own4))]
    up += [up_matrix(list(range(-own4, 2 * own4)), linear(-own4 // 2, 3 * own4 // 2))]
    return down, up


def mm(x, matrix, parts=2):
    heads = []
    for part in range(parts):
        heads.append(x.astype(jnp.bfloat16))
        if part < parts - 1:
            x = x - heads[-1].astype(jnp.float32)
    total = jnp.dot(wide(heads[:2]), matrix, preferred_element_type=jnp.float32)
    if parts == 3:
        total += jnp.dot(heads[2], matrix[: x.shape[1], :], preferred_element_type=jnp.float32)
    return total


def bump(values, anchor):
    offset = values - anchor
    return offset * jnp.exp2(offset * offset * exponent_scale)


def hat(guidance, anchor):
    return jnp.maximum(0.0, 1.0 - jnp.abs(guidance - anchor) * (CHANNELS - 1))


def anchor_of(k):
    return np.float32(k) / np.float32(CHANNELS - 1)


def wide(parts):
    return parts[0] if len(parts) == 1 else jnp.concatenate(parts, axis=1)


def lane(t):
    return slice(t * LANE, (t + 1) * LANE)


def row_down(ref, lead, start, count):
    lead = lead if isinstance(lead, tuple) else (lead,)

    def tap(s):
        return ref[(*lead, pl.ds(start + s - 2, count, stride=2), slice(None))]

    return 0.375 * tap(2) + 0.25 * (tap(1) + tap(3)) + 0.0625 * (tap(0) + tap(4))


def row_up(ref, t, start, count):
    before = ref[t, pl.ds(start - 1, count), :]
    here = ref[t, pl.ds(start, count), :]
    after = ref[t, pl.ds(start + 1, count), :]
    return (before + 6.0 * here + after) * 0.125, (here + after) * 0.5


def turn(x, shift):
    shift %= LANE
    return x if shift == 0 else pltpu.roll(x, shift, 1)


def lanes_of(x):
    return lax.broadcasted_iota(jnp.int32, x.shape, 1)


def pack(x, first):
    count = x.shape[0] // 4
    groups = [turn(x[g * count : (g + 1) * count, :], g * QUARTER - first) for g in range(4)]
    return beside(groups)


def beside(groups):
    result = groups[-1]
    index = lanes_of(result)
    for g in reversed(range(len(groups) - 1)):
        result = jnp.where(index < (g + 1) * QUARTER, groups[g], result)
    return result


def chunk_of(count):
    for size in range(320, 0, -8):
        if count % size == 0:
            return size
    return count


def kernel(axes, spans, gain_hbm, lum_hbm, bank, out, *refs):
    (gain, lum, top, bottom, side_out, side_in, halo, center, remapped, weights, total, result, mats) = refs[:13]
    (g1, g2, g3, g4, e4, g5, u1, u2, u3, u4, v1, v2, v3, v4, c1, c2, c3, c4, c5, packed, gathered) = refs[13:34]
    send_a, recv_a, send_b, recv_b, bank_sem, lum_sem, gain_sem = refs[34:]
    block_rows, block_cols = lum.shape
    own_tiles = block_cols // LANE
    half = block_rows // 2
    counts = [lax.axis_size(a) for a in axes]
    place = [lax.axis_index(a) for a in axes]

    def device(dr, dc):
        return tuple(lax.rem(p + d + n, n) for p, d, n in zip(place, (dr, dc), counts))

    def matrix(name):
        start, depth, count = spans[name]
        whole = wide([mats[start + t * depth : start + (t + 1) * depth, :] for t in range(count)])
        return jnp.concatenate([whole, whole], axis=0)

    barrier = pltpu.get_barrier_semaphore()
    for dr, dc in STEPS:
        pl.semaphore_signal(barrier, inc=1, device_id=device(dr, dc), device_id_type=MESH)
    lum_copy = pltpu.make_async_copy(lum_hbm, lum, lum_sem)
    lum_copy.start()
    gain_copy = pltpu.make_async_copy(gain_hbm, gain, gain_sem)
    gain_copy.start()
    bank_copy = pltpu.make_async_copy(bank, mats, bank_sem)
    bank_copy.start()
    lum_copy.wait()

    mid, corner = block_rows // 4, HALO // 4
    for s, (t, start) in enumerate(((0, 0), (own_tiles - 1, LANE - QUARTER))):
        side_out[s, 0:mid, :] = pack(lum[:, lane(t)], start)
        side_out[s, mid : mid + corner, :] = pack(lum[0:HALO, lane(t)], start)
        side_out[s, mid + corner : mid + 2 * corner, :] = pack(lum[block_rows - HALO :, lane(t)], start)
    pl.semaphore_wait(barrier, len(STEPS))

    rows_at = {0: (0, mid), -1: (mid, corner), 1: (mid + corner, corner)}
    copies = []
    for index, (dr, dc) in enumerate(STEPS):
        if dc == 0:
            src = lum.at[pl.ds(0 if dr < 0 else block_rows - HALO, HALO), :]
            dst = bottom if dr < 0 else top
        else:
            s = 0 if dc < 0 else 1
            src = side_out.at[s, pl.ds(*rows_at[dr]), :]
            dst = side_in.at[1 - s, pl.ds(*rows_at[-dr]), :]
        copy = pltpu.make_async_remote_copy(
            src_ref=src,
            dst_ref=dst,
            send_sem=send_a.at[index],
            recv_sem=recv_a.at[index],
            device_id=device(dr, dc),
            device_id_type=MESH,
        )
        copy.start()
        copies.append(copy)
    for t in range(own_tiles):
        center[t, :, :] = lum[:, lane(t)]
    total[...] = jnp.zeros_like(total)

    def own_cells(t, carry):
        for r in range(0, block_rows, 32):
            values = center[t, r : r + 32, :]
            remapped[CHANNELS, t, PAD + HALO + r : PAD + HALO + r + 32, :] = values
            running = 0.5 * values
            for k in range(CHANNELS):
                value, weight = bump(values, anchor_of(k)), hat(values, anchor_of(k))
                remapped[k, t, PAD + HALO + r : PAD + HALO + r + 32, :] = value
                weights[k, t, r : r + 32, :] = weight
                running = running + weight * value
            result[t, r : r + 32, :] = running
        return carry

    lax.fori_loop(0, own_tiles, own_cells, 0)
    for copy in copies:
        copy.wait()
    bank_copy.wait()
    gain_copy.wait()

    ext_rows = block_rows + 2 * HALO
    for start, (at, count) in ((0, rows_at[-1]), (HALO, rows_at[0]), (HALO + block_rows, rows_at[1])):
        left, right = side_in[0, at : at + count, :], side_in[1, at : at + count, :]
        index = lanes_of(left)
        for g in range(4):
            halo[start + g * count : start + (g + 1) * count, :] = jnp.where(
                index < LANE // 2, turn(right, -g * QUARTER), turn(left, LANE - QUARTER - g * QUARTER)
            )

    def beyond(t):
        if t == own_tiles:
            return [(r, halo[r : r + 64, :]) for r in range(0, ext_rows, 64)]
        return [(0, top[:, lane(t)]), (HALO + block_rows, bottom[:, lane(t)])]

    rows1 = ext_rows // 2
    tiles1 = g1.shape[0]
    coarse_at = PAD + HALO // 2

    def finest_down(members, dst_row, prepare):
        for k in members:
            for t in range(own_tiles + 1):
                for r, values in beyond(t):
                    remapped[k, t, PAD + r : PAD + r + values.shape[0], :] = prepare(values, k)
        x = [
            wide([row_down(remapped, (k, t), PAD, rows1) for t in range(own_tiles + 1)])
            for k in members
        ]
        y = mm(jnp.concatenate(x, axis=0), matrix("d0"))
        for t in range(tiles1):
            g1[t, pl.ds(dst_row, len(members) * rows1), :] = y[:, lane(t)]

    def prepared(values, k):
        return values if k == CHANNELS else bump(values, anchor_of(k))

    finest_down(list(range(GROUP)), PAD, prepared)
    finest_down(list(range(GROUP, STACK)), PAD + GROUP * rows1, prepared)

    def finest_up(members):
        x = []
        for k in members:
            pairs = [row_up(g1, t, coarse_at + k * rows1, half) for t in range(tiles1)]
            x += [wide([p[0] for p in pairs]), wide([p[1] for p in pairs])]
        fine = mm(jnp.concatenate(x, axis=0), matrix("u0"))
        for t in range(own_tiles):
            for p in range(2):
                running = total[t, p * half : (p + 1) * half, :]
                for q, k in enumerate(members):
                    at = (2 * q + p) * half
                    weight = 0.5 if k == CHANNELS else weights[k, t, pl.ds(p, half, stride=2), :]
                    running = running + weight * fine[at : at + half, lane(t)]
                total[t, p * half : (p + 1) * half, :] = running

    def shrink(src, dst, name, count):
        step = chunk_of(count)
        for o in range(0, count, step):
            x = wide([row_down(src, t, PAD + 2 * o, step) for t in range(src.shape[0])])
            y = mm(x, matrix(name))
            for t in range(dst.shape[0]):
                dst[t, PAD + o : PAD + o + step, :] = y[:, lane(t)]

    rows2, rows3, rows4 = rows1 // 2, rows1 // 4, rows1 // 8
    shrink(g1, g2, "d1", STACK * rows2)
    shrink(g2, g3, "d2", STACK * rows3)
    shrink(g3, g4, "d3", STACK * rows4)

    own4 = block_rows // 16
    skip4 = HALO // 16
    groups = -(-STACK // 4)
    for g in range(groups):
        members = []
        for q in range(4):
            k = min(4 * g + q, CHANNELS)
            at = PAD + k * rows4 + skip4
            members.append(turn(g4[0, at : at + own4, :], q * QUARTER))
        packed[g * own4 : (g + 1) * own4, :] = beside(members)
    copies = []
    for index, (dr, dc) in enumerate(STEPS):
        copy = pltpu.make_async_remote_copy(
            src_ref=packed,
            dst_ref=gathered.at[len(STEPS) - 1 - index],
            send_sem=send_b.at[index],
            recv_sem=recv_b.at[index],
            device_id=device(dr, dc),
            device_id_type=MESH,
        )
        copy.start()
        copies.append(copy)

    def detail(level, fine_stack, coarse_stack, spread, wider, name, fine, coarse, skip, a, b):
        count = STACK * coarse
        step = chunk_of(count)
        for o in range(0, count, step):
            for t in range(coarse_stack.shape[0]):
                even, odd = row_up(coarse_stack, t, PAD + o, step)
                spread[t, pl.ds(2 * o, step, stride=2), :] = even
                spread[t, pl.ds(2 * o + 1, step, stride=2), :] = odd
            x = wide([spread[t, 2 * o : 2 * (o + step), :] for t in range(coarse_stack.shape[0])])
            y = mm(x, matrix(name))
            for t in range(fine_stack.shape[0]):
                wider[t, 2 * o : 2 * (o + step), :] = y[:, lane(t)]
        sums = []
        for t in range(fine_stack.shape[0]):

            def difference(k):
                at = k * 2 * coarse + skip
                return (
                    fine_stack[t, PAD + k * fine + a : PAD + k * fine + b, :]
                    - wider[t, at + a : at + b, :]
                )

            guidance = fine_stack[t, PAD + CHANNELS * fine + a : PAD + CHANNELS * fine + b, :]
            running = 0.5 * difference(CHANNELS)
            for k in range(CHANNELS):
                running = running + hat(guidance, anchor_of(k)) * difference(k)
            sums.append(gain[level] * running)
        return sums

    for k in range(0, CHANNELS, 4):
        finest_up(list(range(k, STACK if k + 4 == CHANNELS else k + 4)))
    near = HALO // 2 - 8
    coef1 = detail(1, g1, g2, u1, v1, "u1", rows1, rows2, 0, near, rows1 - near)
    coef2 = detail(2, g2, g3, u2, v2, "u2", rows2, rows3, 0, 0, rows2)

    for copy in copies:
        copy.wait()
    for k in range(STACK):
        g, q = divmod(k, 4)
        for dr in (-1, 0, 1):
            members = []
            for dc in (-1, 0, 1):
                if (dr, dc) == (0, 0):
                    piece = packed[g * own4 : (g + 1) * own4, :]
                else:
                    piece = gathered[STEPS.index((dr, dc)), g * own4 : (g + 1) * own4, :]
                members.append(turn(piece, (dc + 1 - q) * QUARTER))
            at = PAD + (3 * k + dr + 1) * own4
            e4[0, at : at + own4, :] = beside(members)

    ext4 = 3 * own4
    ext5 = ext4 // 2
    shrink(e4, g5, "d4", STACK * ext5)
    coef3 = detail(3, g3, e4, u3, v3, "u3", rows3, ext4, 2 * (own4 - skip4), 0, rows3)
    coef4 = detail(4, e4, g5, u4, v4, "u4", ext4, ext5, 0, 0, ext4)

    guide_at = PAD + CHANNELS * ext5
    c5[0, PAD : PAD + ext5, :] = g5[0, guide_at : guide_at + ext5, :]

    def collapse(coarse, start, fine, at, coefficients, name):
        count = coefficients[0].shape[0] // 2
        for t in range(coarse.shape[0]):
            even, odd = row_up(coarse, t, PAD + start, count)
            u1[t, pl.ds(0, count, stride=2), :] = even
            u1[t, pl.ds(1, count, stride=2), :] = odd
        y = mm(wide([u1[t, 0 : 2 * count, :] for t in range(coarse.shape[0])]), matrix(name), 3)
        for t in range(fine.shape[0]):
            fine[t, PAD + at : PAD + at + 2 * count, :] = coefficients[t] + y[:, lane(t)]

    collapse(c5, 0, c4, 0, coef4, "u4")
    collapse(c4, own4 - skip4, c3, 0, coef3, "u3")
    collapse(c3, 0, c2, 0, coef2, "u2")
    collapse(c2, near // 2, c1, near, coef1, "u1")
    pairs = [row_up(c1, t, coarse_at, half) for t in range(tiles1)]
    x = jnp.concatenate([wide([p[0] for p in pairs]), wide([p[1] for p in pairs])], axis=0)
    fine = mm(x, matrix("u0"), 3)
    for t in range(own_tiles):
        for p in range(2):
            own = result[t, pl.ds(p, half, stride=2), :] - total[t, p * half : (p + 1) * half, :]
            result[t, pl.ds(p, half, stride=2), :] = (
                gain[0] * own + fine[p * half : (p + 1) * half, lane(t)]
            )
        out[:, lane(t)] = result[t, :, :]


def tone(axes, luminance, level_gain):
    block_rows, block_cols = luminance.shape
    down, up = matrices(block_cols)
    spans, parts, start = {}, [], 0
    for prefix, group in (("d", down), ("u", up)):
        for level, m in enumerate(group):
            count = m.shape[1] // LANE
            spans[prefix + str(level)] = (start, m.shape[0], count)
            parts += [m[:, lane(t)] for t in range(count)]
            start += m.shape[0] * count
    bank = jnp.asarray(np.concatenate(parts), jnp.bfloat16)

    def f32(*shape):
        return pltpu.VMEM(shape, jnp.float32)

    def stack(tiles, count):
        return f32(tiles, ceil_to(count, 8) + 2 * PAD, LANE)

    own_tiles = block_cols // LANE
    tiles = [-(-len(circle(block_cols, l)) // LANE) for l in range(4)] + [1, 1]
    ext = block_rows + 2 * HALO
    rows = [ext >> l for l in range(5)]
    own4 = block_rows // 16
    ext4, ext5 = 3 * own4, 3 * own4 // 2
    side = block_rows // 4 + HALO // 2
    scratch = [
        pltpu.SMEM(level_gain.shape, jnp.float32),
        f32(block_rows, block_cols),
        f32(HALO, block_cols),
        f32(HALO, block_cols),
        f32(2, side, LANE),
        f32(2, side, LANE),
        f32(ext, LANE),
        f32(own_tiles, block_rows, LANE),
        f32(STACK, own_tiles + 1, ext + 2 * PAD, LANE),
        f32(CHANNELS, own_tiles, block_rows, LANE),
        f32(own_tiles, block_rows, LANE),
        f32(own_tiles, block_rows, LANE),
        pltpu.VMEM(bank.shape, jnp.bfloat16),
        stack(tiles[1], STACK * rows[1]),
        stack(tiles[2], STACK * rows[2]),
        stack(tiles[3], STACK * rows[3]),
        stack(1, STACK * rows[4]),
        stack(1, STACK * ext4),
        stack(1, STACK * ext5),
        stack(tiles[2], STACK * rows[1]),
        stack(tiles[3], STACK * rows[2]),
        stack(1, STACK * 2 * ext4),
        stack(1, STACK * ext4),
        stack(tiles[1], STACK * rows[1]),
        stack(tiles[2], STACK * rows[2]),
        stack(tiles[3], STACK * 2 * ext4),
        stack(1, STACK * ext4),
        stack(tiles[1], rows[1]),
        stack(tiles[2], rows[2]),
        stack(tiles[3], rows[3]),
        stack(1, ext4),
        stack(1, ext5),
        f32(-(-STACK // 4) * own4, LANE),
        f32(len(STEPS), -(-STACK // 4) * own4, LANE),
    ]
    dma = pltpu.SemaphoreType.DMA
    scratch += [dma((8,)), dma((8,)), dma((8,)), dma((8,)), dma, dma, dma]
    vmem = pl.BlockSpec(memory_space=pltpu.VMEM)
    hbm = pl.BlockSpec(memory_space=pltpu.HBM)
    return pl.pallas_call(
        functools.partial(kernel, axes, spans),
        out_shape=jax.ShapeDtypeStruct((block_rows, block_cols), jnp.float32),
        in_specs=[hbm, hbm, hbm],
        out_specs=vmem,
        scratch_shapes=scratch,
        compiler_params=pltpu.CompilerParams(
            vmem_limit_bytes=56 * 1024 * 1024, collective_id=0, has_side_effects=True
        ),
        name="tone_pyramid",
    )(level_gain, luminance, bank)


def solution(mesh):
    placed = (P("row", "col"), P())

    def local(luminance, level_gain):
        return tone(("row", "col"), luminance, level_gain)

    return jax.shard_map(
        local, mesh=mesh, in_specs=placed, out_specs=P("row", "col"), check_vma=False
    )
```
